128 devices in a mesh: wn: 8 (over x, core), xz: 16 (over y, z).
Axes of the slice: x: 4, y: 4, z: 4, core: 2. Of those that a mesh axis runs over, the one named last changes fastest.
Arguments:
- velocity: float32 [3, 1024, 32, 2048], P(None, 'wn', None, 'xz'), may hold values from -3.5 to 3.5
- viscosity: float32 [1024, 32, 2048], P('wn', None, 'xz'), may hold values from 2 to 10
Outputs:
- new_velocity: float32 [3, 1024, 32, 2048], P(None, 'wn', None, 'xz')
The draws below stay inside these ranges and needn't reach their ends.
All inputs are finite; a program needn't handle non-finite values.
Results may differ from the reference program's by a relative error of at most 0.0003.
Values sent between devices are 32-bit elements; how exact they have to be, the bound alone decides.
No kernel may reach another device: no remote copies, remote signals or barrier semaphores. Data moves between devices by JAX's collectives and lax.ppermute only.
A program may use at most 192 MiB of HBM per device.

```python
import math
import jax
import jax.numpy as jnp
from jax import lax

NX = 32
NY = 1024
NZ = 2048


def draw_velocity(key, part):
    key = jax.random.fold_in(key, 11)
    first_key = jax.random.fold_in(key, 0)
    third_key = jax.random.fold_in(key, 2)
    fourth_key = jax.random.fold_in(key, 3)
    height = (jnp.arange(NY, dtype=jnp.float32) + 0.5) / NY
    profile = (6.0 * height * (1.0 - height)).reshape(1, NY, 1, 1)
    swing = jnp.sin(6.283185307 * height).reshape(1, NY, 1, 1)
    line_scale = jax.random.uniform(third_key, (1, 1, NX, NZ), jnp.float32, 0.4, 1.6)
    line_tilt = jax.random.uniform(fourth_key, (3, 1, NX, NZ), jnp.float32, -0.6, 0.6)
    weights = jnp.array([1.5, 0.0, 0.0], jnp.float32).reshape(3, 1, 1, 1)
    rough = jnp.clip(jax.random.normal(first_key, (3, NY, NX, NZ), jnp.float32) * 0.5, -1.25, 1.25)
    smooth = weights * line_scale * profile + line_tilt * swing
    return jnp.clip(smooth + rough, -3.5, 3.5)


def shard_levels(own_key, dims, cuts, least, largest):
    level = 1.0
    for dim, blocks in cuts:
        steps = jax.random.uniform(jax.random.fold_in(jax.random.fold_in(own_key, 6), dim), (blocks,), jnp.float32, least / len(cuts), largest / len(cuts))
        level = level * jnp.repeat(jnp.exp(steps), dims[dim] // blocks).reshape((-1,) + (1,) * (len(dims) - 1 - dim))
    return level


def setup_inputs(seed: int = 0) -> dict:
    splits = jax.random.split(jax.random.key(seed), 3)
    return {
        "velocity": draw_velocity(jax.random.fold_in(splits[2], 71), 0),
        "viscosity": jnp.clip(jnp.exp(math.log(10.0) - 1.609438 * jax.random.uniform(splits[1], (NY, NX, NZ), jnp.float32) ** shard_levels(splits[1], (NY, NX, NZ), ((0, 8), (2, 16)), -0.2, 0.2)), 2.0, 10.0),
    }


x_courant = 0.25
y_courant = 0.5
z_courant = 0.25
diffusion_rate = 2000.0


def advect(velocity, diff_x, diff_y, diff_z):
    return velocity - (x_courant * velocity[0] * diff_x + y_courant * velocity[1] * diff_y + z_courant * velocity[2] * diff_z)


def line_solve(rhs, lower_rate, upper_rate):
    rhs_rows = jnp.moveaxis(rhs, 1, 0)

    def forward(state, inputs):
        ratios, values = state
        source, lower_face, upper_face = inputs
        pivots = (1.0 + lower_face + upper_face) + lower_face * ratios
        new_ratios = -upper_face / pivots
        new_values = (source + lower_face * values) / pivots
        return (new_ratios, new_values), (new_ratios, new_values)

    start_state = (jnp.zeros(lower_rate.shape[1:], jnp.float32), jnp.zeros(rhs_rows.shape[1:], jnp.float32))
    _, (all_ratios, all_values) = lax.scan(forward, start_state, (rhs_rows, lower_rate, upper_rate))

    def backward(following, inputs):
        ratios, values = inputs
        result = values - ratios * following
        return result, result

    _, solved = lax.scan(backward, jnp.zeros(rhs_rows.shape[1:], jnp.float32), (all_ratios, all_values), reverse=True)
    return jnp.moveaxis(solved, 0, 1)


def reference(velocity, viscosity):
    diff_x = jnp.roll(velocity, -1, 2) - jnp.roll(velocity, 1, 2)
    padded = jnp.pad(velocity, ((0, 0), (1, 1), (0, 0), (0, 0)))
    diff_y = padded[:, 2:] - padded[:, :-2]
    diff_z = jnp.roll(velocity, -1, 3) - jnp.roll(velocity, 1, 3)
    rhs = advect(velocity, diff_x, diff_y, diff_z)
    extended = jnp.concatenate([viscosity[:1], viscosity, viscosity[-1:]], 0)
    lower_rate = diffusion_rate * 0.5 * (viscosity + extended[:-2])
    upper_rate = diffusion_rate * 0.5 * (viscosity + extended[2:])
    return line_solve(rhs, lower_rate, upper_rate)
```

```python
import functools

import jax
import jax.numpy as jnp
from jax import lax
from jax.experimental import pallas as pl
from jax.experimental.pallas import tpu as pltpu
from jax.sharding import PartitionSpec as P

x_courant = 0.25
y_courant = 0.5
z_courant = 0.25
face_rate = 1000.0

SUB = 8
LANES = 128
VMEM = pltpu.VMEM
f32 = jnp.float32
bf16 = jnp.bfloat16


def lane_index():
    return lax.broadcasted_iota(jnp.int32, (SUB, LANES), 1)


def sub_index():
    return lax.broadcasted_iota(jnp.int32, (SUB, LANES), 0)


def tile(ref, *lead, t):
    return ref[(*lead, pl.ds(t * SUB, SUB), slice(None))]


def put(ref, value, *lead, t):
    ref[(*lead, pl.ds(t * SUB, SUB), slice(None))] = value


def square(ref, *lead, start, nx):
    rows = LANES // nx
    return ref[(*lead, pl.ds(start, rows))].reshape(LANES, LANES)


def head_kernel(
    chunk, vel_hbm, visc_hbm, marks, vel, low, high, row_out, row_in, wid, hid, rec, fwd, flags, visc, sems
):
    comps, rows, nx, _ = vel_hbm.shape
    tiles = nx // SUB
    group = LANES // nx
    chunks = rows // chunk

    def visc_copy(k):
        span = pl.ds(k * chunk, chunk)
        return pltpu.make_async_copy(visc_hbm.at[span], visc.at[span], sems.at[0, k])

    def vel_copy(k):
        span = pl.ds(k * chunk, chunk)
        inner = pl.ds(k * chunk + 1, chunk)
        return pltpu.make_async_copy(vel_hbm.at[:, span], vel.at[:, inner], sems.at[1, k])

    for k in range(chunks):
        visc_copy(k).start()
    for k in range(chunks):
        vel_copy(k).start()
    flags[...] = marks[...]
    zero = jnp.zeros((SUB, LANES), f32)
    for c in range(comps):
        for t in range(tiles):
            put(vel, zero, c, 0, t=t)
            put(vel, zero, c, rows + 1, t=t)
    wall_low = jnp.broadcast_to(marks[1:2, :], (SUB, LANES))
    wall_high = jnp.broadcast_to(marks[2:3, :], (SUB, LANES))

    def body(k, state, last=False):
        if not last:
            visc_copy(k + 1).wait()
        vel_copy(k).wait()
        state = list(state)
        for r in range(chunk):
            y = k * chunk + r
            end = last and r == chunk - 1
            for t in range(tiles):
                extra, cell, face, reach = state[4 * t : 4 * t + 4]
                inner = 1.0 + extra
                if end:
                    next_cell = cell
                    next_face = wall_high * (2.0 * cell)
                else:
                    next_cell = face_rate * tile(visc, y + 1, t=t)
                    next_face = cell + next_cell
                r_ = pltpu.reciprocal(inner + next_face, approx=False)
                w = r_ if end else next_face * r_
                h = face * r_
                reach = h * reach
                put(wid, w, y, t=t)
                put(hid, h, y, t=t)
                put(rec, r_, y, t=t)
                put(fwd, reach, y, t=t)
                state[4 * t : 4 * t + 4] = [w * inner, next_cell, next_face, reach]
            if r % group == group - 1:
                start = k * chunk + r - group + 1
                spot = (k * chunk + r) // group
                for c in range(comps):
                    turned = square(vel, c, start=start + 1, nx=nx).T
                    low[c, pl.ds(spot, 1), :] = turned[:1]
                    high[c, pl.ds(spot, 1), :] = turned[LANES - 1 :]
        return tuple(state)

    visc_copy(0).wait()
    state = []
    one = jnp.ones((SUB, LANES), f32)
    for t in range(tiles):
        cell = face_rate * tile(visc, 0, t=t)
        state += [wall_low * (2.0 * cell), cell, one, one]
    state = lax.fori_loop(0, chunks - 1, body, tuple(state))
    body(chunks - 1, state, last=True)

    upper = jnp.broadcast_to(marks[0:1, :], (SUB, LANES)) > 0.5
    for c in range(comps + 1):
        for t in range(tiles):
            if c < comps:
                first, end = tile(vel, c, 1, t=t), tile(vel, c, rows, t=t)
            else:
                first, end = tile(visc, 0, t=t), tile(visc, rows - 1, t=t)
            put(row_out, jnp.where(upper, end, first), c, t=t)
            put(row_in, jnp.where(upper, first, end), c, t=t)


def shifted(ref, lead, t, tiles, forward, sub):
    if forward:
        if t < tiles - 1:
            return ref[(*lead, pl.ds(t * SUB + 1, SUB), slice(None))]
        mixed = jnp.where(sub == 0, tile(ref, *lead, t=0), tile(ref, *lead, t=t))
        return pltpu.roll(mixed, SUB - 1, 0)
    if t > 0:
        return ref[(*lead, pl.ds(t * SUB - 1, SUB), slice(None))]
    mixed = jnp.where(sub == SUB - 1, tile(ref, *lead, t=tiles - 1), tile(ref, *lead, t=t))
    return pltpu.roll(mixed, 1, 0)


def block_kernel(vel, wid, rec, fwd, rhs, left, right, ends, dots, edges, buf_a, buf_b):
    comps, rows, nx, _ = rhs.shape
    tiles = nx // SUB
    group = LANES // nx
    groups = rows // group
    sub = sub_index()
    a = lax.broadcasted_iota(jnp.int32, (2 * LANES, LANES), 0) % LANES
    b = lax.broadcasted_iota(jnp.int32, (2 * LANES, LANES), 1)
    ahead = (a == (b + 1) % LANES).astype(f32)
    behind = (a == (b + LANES - 1) % LANES).astype(f32)
    central = (z_courant * (ahead - behind)).astype(bf16)

    def differ(buf, g):
        for c in range(comps):
            whole = square(vel, c, start=g * group + 1, nx=nx)
            coarse = whole.astype(bf16)
            fine = (whole - coarse.astype(f32)).astype(bf16)
            buf[c] = jnp.dot(jnp.concatenate([coarse, fine], 1), central, preferred_element_type=f32)

    def process(g, buf, state):
        state = list(state)
        for r in reversed(range(group)):
            y = g * group + r
            for t in range(tiles):
                ul, ur, *sums = state[8 * t : 8 * t + 8]
                w = tile(wid, y, t=t)
                ul, ur = tile(fwd, y, t=t) + w * ul, w * ur
                put(left, ul, y, t=t)
                put(right, ur, y, t=t)
                mid = [tile(vel, c, y + 1, t=t) for c in range(comps)]
                rate_x, rate_y = x_courant * mid[0], y_courant * mid[1]
                for c in range(comps):
                    lead = (c, y + 1)
                    diff_x = shifted(vel, lead, t, tiles, True, sub) - shifted(vel, lead, t, tiles, False, sub)
                    diff_y = tile(vel, c, y + 2, t=t) - tile(vel, c, y, t=t)
                    diff_z = buf[c, pl.ds(r * nx + t * SUB, SUB), :]
                    source = mid[c] - (rate_x * diff_x + rate_y * diff_y + mid[2] * diff_z)
                    put(rhs, source, c, y, t=t)
                    sums[c] = sums[c] + ul * source
                    sums[comps + c] = sums[comps + c] + ur * source
                state[8 * t : 8 * t + 8] = [ul, ur, *sums]
        return tuple(state)

    def pack(g):
        for k, ref in enumerate((left, right)):
            turned = square(ref, start=g * group, nx=nx).T
            edges[2 * k, pl.ds(g, 1), :] = turned[:1]
            edges[2 * k + 1, pl.ds(g, 1), :] = turned[LANES - 1 :]

    def body(m, state):
        g = groups - 1 - 2 * m
        differ(buf_b, g - 1)
        state = process(g, buf_a, state)
        pack(jnp.minimum(g + 1, groups - 1))
        differ(buf_a, jnp.maximum(g - 2, 0))
        state = process(g - 1, buf_b, state)
        pack(g)
        return state

    zero, one = jnp.zeros((SUB, LANES), f32), jnp.ones((SUB, LANES), f32)
    differ(buf_a, groups - 1)
    state = ([zero, one] + [zero] * 6) * tiles
    state = lax.fori_loop(0, groups // 2, body, tuple(state))
    pack(0)
    for t in range(tiles):
        ul, ur, *sums = state[8 * t : 8 * t + 8]
        put(ends, ul, 0, t=t)
        put(ends, tile(fwd, rows - 1, t=t), 1, t=t)
        put(ends, tile(rec, rows - 1, t=t), 2, t=t)
        for k in range(6):
            put(dots, sums[k], k, t=t)


def edge_kernel(low, high, from_left, from_right, edges, dots, edge_low, edge_high, values):
    comps, groups, _ = low.shape
    _, nx, _ = dots.shape
    lane, sub = lane_index(), sub_index()
    edge_low[...] = z_courant * low[2] * (from_left[...] - high[...])
    edge_high[...] = -z_courant * high[2] * (from_right[...] - low[...])
    for k in range(2):
        for c in range(comps):
            line_low = jnp.sum(edges[2 * k] * edge_low[c], 0, keepdims=True)
            line_high = jnp.sum(edges[2 * k + 1] * edge_high[c], 0, keepdims=True)
            for t in range(nx // SUB):
                mine = lane % nx == sub + t * SUB
                at_low = jnp.sum(jnp.where(mine, line_low, 0.0), 1, keepdims=True)
                at_high = jnp.sum(jnp.where(mine, line_high, 0.0), 1, keepdims=True)
                add = jnp.where(lane == 0, at_low, jnp.where(lane == LANES - 1, at_high, 0.0))
                put(values, tile(dots, comps * k + c, t=t) + add, comps * k + c, t=t)


def sweep_kernel(rhs, low, high, wid, hid, rec, out, buf_a, buf_b):
    comps, rows, nx, _ = rhs.shape
    tiles = nx // SUB
    group = LANES // nx
    groups = rows // group
    sub = sub_index()
    zero = jnp.zeros((SUB, LANES), f32)
    middle = jnp.zeros((LANES - 2 * SUB, LANES), f32)

    def spread(buf, g):
        for c in range(comps):
            top = jnp.where(sub == 0, low[c, pl.ds(g, 1), :], 0.0)
            bottom = jnp.where(sub == SUB - 1, high[c, pl.ds(g, 1), :], 0.0)
            buf[c] = jnp.concatenate([top, middle, bottom], 0).T

    def process(g, buf, state):
        new = list(state)
        for r in range(group):
            y = g * group + r
            for t in range(tiles):
                r_, h = tile(rec, y, t=t), tile(hid, y, t=t)
                for c in range(comps):
                    k = t * comps + c
                    source = tile(rhs, c, y, t=t) + buf[c, pl.ds(r * nx + t * SUB, SUB), :]
                    new[k] = source * r_ + h * new[k]
                    put(out, new[k], c, y, t=t)
        return tuple(new)

    def forward(m, state):
        g = 2 * m
        spread(buf_b, g + 1)
        state = process(g, buf_a, state)
        spread(buf_a, jnp.minimum(g + 2, groups - 1))
        return process(g + 1, buf_b, state)

    spread(buf_a, 0)
    lax.fori_loop(0, groups // 2, forward, (zero,) * (comps * tiles))

    def backward(k, state):
        y = rows - 1 - k
        new = list(state)
        for t in range(tiles):
            w = tile(wid, y, t=t)
            for c in range(comps):
                k = t * comps + c
                new[k] = tile(out, c, y, t=t) + w * state[k]
                put(out, new[k], c, y, t=t)
        return tuple(new)

    lax.fori_loop(0, rows, backward, (zero,) * (comps * tiles), unroll=4)


def finish_kernel(chunks, part, left, right, flux, out_hbm, out, sems):
    comps, rows, nx, _ = part.shape
    tiles = nx // SUB
    step = rows // chunks

    copies = []
    for k in range(chunks):
        for t in range(tiles):
            fl = [tile(flux, c, t=t) for c in range(comps)]
            fr = [tile(flux, comps + c, t=t) for c in range(comps)]

            def row(y, carry):
                ul, ur = tile(left, y, t=t), tile(right, y, t=t)
                for c in range(comps):
                    put(out, tile(part, c, y, t=t) + (ul * fl[c] + ur * fr[c]), c, y, t=t)
                return carry

            lax.fori_loop(k * step, (k + 1) * step, row, 0, unroll=4)
        span = pl.ds(k * step, step)
        copies.append(pltpu.make_async_copy(out.at[:, span], out_hbm.at[:, span], sems.at[k]))
        copies[-1].start()
    for copy in copies:
        copy.wait()


def vmem_out(*shape):
    return VMEM(shape, f32)


def in_vmem(n):
    return [pl.BlockSpec(memory_space=VMEM)] * n


def cost(flops, moved):
    return pl.CostEstimate(flops=flops, bytes_accessed=moved, transcendentals=0)


def local(velocity, viscosity):
    comps, rows, nx, nz = velocity.shape
    cells = rows * nx * nz
    groups = rows * nx // LANES
    hbm = pl.BlockSpec(memory_space=pltpu.HBM)
    params = pltpu.CompilerParams(vmem_limit_bytes=8 * 2**20)

    wn = lax.axis_index("wn")
    count = lax.axis_size("wn")
    planes = lax.axis_size("xz")
    chip, core = wn // 2, wn % 2
    marks = [
        core == 1,
        wn == 0,
        wn == count - 1,
        (core == 1) == (chip % 2 == 0),
        (chip == 1) | (chip == 2),
    ]
    marks = [jnp.full((1, LANES), 1.0, f32) * mark.astype(f32) for mark in marks]
    marks = jnp.concatenate(marks + [jnp.zeros((SUB - len(marks), LANES), f32)], 0)

    chunk = 16
    vel, low, high, row_out, row_in, wid, hid, rec, fwd, flags = pl.pallas_call(
        functools.partial(head_kernel, chunk),
        out_shape=(
            vmem_out(comps, rows + 2, nx, nz),
            vmem_out(comps, groups, LANES),
            vmem_out(comps, groups, LANES),
            vmem_out(comps + 1, nx, nz),
            vmem_out(comps + 1, nx, nz),
            vmem_out(rows, nx, nz),
            vmem_out(rows, nx, nz),
            vmem_out(rows, nx, nz),
            vmem_out(rows, nx, nz),
            vmem_out(SUB, LANES),
        ),
        in_specs=[hbm, hbm] + in_vmem(1),
        out_specs=in_vmem(10),
        scratch_shapes=[VMEM((rows, nx, nz), f32), pltpu.SemaphoreType.DMA((2, rows // chunk))],
        compiler_params=pltpu.CompilerParams(vmem_limit_bytes=42 * 2**20),
        name="head",
    )(velocity, viscosity, marks)

    with jax.named_scope("halo_z"):
        from_left = lax.ppermute(high, "xz", [(i, (i + 1) % planes) for i in range(planes)])
        from_right = lax.ppermute(low, "xz", [((i + 1) % planes, i) for i in range(planes)])
    with jax.named_scope("halo_y"):
        pairs = [(i, (i + 1) % count if i % 2 else (i - 1) % count) for i in range(count)]
        row_other = lax.ppermute(row_out, "wn", pairs)

    rhs, left, right, ends, dots, edges = pl.pallas_call(
        block_kernel,
        out_shape=(
            vmem_out(comps, rows, nx, nz),
            vmem_out(rows, nx, nz),
            vmem_out(rows, nx, nz),
            vmem_out(3, nx, nz),
            vmem_out(2 * comps, nx, nz),
            vmem_out(4, groups, LANES),
        ),
        in_specs=in_vmem(4),
        out_specs=in_vmem(6),
        scratch_shapes=[VMEM((comps, LANES, LANES), f32)] * 2,
        compiler_params=params,
        cost_estimate=cost(60 * cells, 40 * cells),
        name="block",
    )(vel, wid, rec, fwd)

    edge_low, edge_high, values = pl.pallas_call(
        edge_kernel,
        out_shape=(
            vmem_out(comps, groups, LANES),
            vmem_out(comps, groups, LANES),
            vmem_out(2 * comps, nx, nz),
        ),
        in_specs=in_vmem(6),
        out_specs=in_vmem(3),
        compiler_params=params,
        name="edge",
    )(low, high, from_left, from_right, edges, dots)

    upper_core, first_block, last_block, in_near, middle = (flags[k : k + 1] > 0.5 for k in range(5))
    value_first, value_last = values[:comps], values[comps:]

    cross = ends[1]
    own_out = jnp.where(upper_core, ends[2], ends[0])
    own_in = jnp.where(upper_core, ends[0], ends[2])
    value_out = jnp.where(upper_core, value_last, value_first)
    value_in = jnp.where(upper_core, value_first, value_last)
    sign_in = jnp.where(upper_core, y_courant, -y_courant)
    push_out = jnp.where(first_block | last_block, 0.0, -sign_in * row_out[1] * row_other[:comps])
    face_out = face_rate * (row_out[3] + row_other[3])
    value_out = value_out + own_out * push_out
    value_in = value_in + cross * push_out

    send = jnp.concatenate(
        [jnp.stack([own_out, cross, own_in]), value_out, value_in, row_in, face_out[None]], 0
    )
    with jax.named_scope("exchange_core"):
        got = lax.ppermute(send, "wn", [(i, i ^ 1) for i in range(count)])
    far_out, far_cross, far_in = got[0], got[1], got[2]
    far_value_out, far_value_in = got[3:6], got[6:9]
    far_row, far_face = got[9:13], got[13]
    push_in = sign_in * row_in[1] * far_row[:comps]
    far_push = -sign_in * far_row[1] * row_in[:comps]
    near_value_in = value_in + own_in * push_in
    near_value_out = value_out + cross * push_in
    far_value_out = far_value_out + far_cross * far_push
    far_value_in = far_value_in + far_in * far_push
    join_core = 1.0 / (1.0 / (face_rate * (row_in[3] + far_row[3])) + own_in + far_in)
    flow = join_core * (far_value_in - near_value_in)
    near_near = own_out - cross * cross * join_core
    near_far = cross * far_cross * join_core
    far_far = far_out - far_cross * far_cross * join_core
    near_value = near_value_out + cross * flow
    far_value = far_value_out - far_cross * flow

    chip_in = jnp.where(in_near, near_near, far_far)
    chip_out = jnp.where(in_near, far_far, near_near)
    chip_value_in = jnp.where(in_near, near_value, far_value)
    chip_value_out = jnp.where(in_near, far_value, near_value)
    chip_face_in = jnp.where(in_near, face_out, far_face)
    chip_face_out = jnp.where(in_near, far_face, face_out)
    send = jnp.concatenate(
        [jnp.stack([chip_out, near_far, chip_in, chip_face_out]), chip_value_out, chip_value_in], 0
    )
    with jax.named_scope("exchange_chip"):
        got = lax.ppermute(send, "wn", [(i, i ^ 2) for i in range(count)])

    part = pl.pallas_call(
        sweep_kernel,
        out_shape=vmem_out(comps, rows, nx, nz),
        in_specs=in_vmem(6),
        out_specs=pl.BlockSpec(memory_space=VMEM),
        scratch_shapes=[VMEM((comps, LANES, LANES), f32)] * 2,
        compiler_params=params,
        cost_estimate=cost(30 * cells, 30 * cells),
        name="sweep",
    )(rhs, edge_low, edge_high, wid, hid, rec)

    other_out, other_cross, other_in, other_face = got[0], got[1], got[2], got[3]
    other_value_out, other_value_in = got[4:7], got[7:10]
    join_chip = 1.0 / (1.0 / chip_face_in + chip_in + other_in)
    flow = join_chip * (other_value_in - chip_value_in)
    half_own = jnp.where(
        middle, chip_out - near_far * near_far * join_chip, other_out - other_cross * other_cross * join_chip
    )
    half_value = jnp.where(middle, chip_value_out + near_far * flow, other_value_out - other_cross * flow)
    half_face = jnp.where(middle, chip_face_out, other_face)
    send = jnp.concatenate([half_own[None], half_value], 0)
    with jax.named_scope("exchange_half"):
        got = lax.ppermute(send, "wn", [(i, i ^ 6) for i in range(count)])
    flow_half = (got[1:] - half_value) / (1.0 / half_face + half_own + got[0])

    flow_out = jnp.where(middle, flow_half, 0.0)
    flow_in = join_chip * (
        other_value_in
        - chip_value_in
        + jnp.where(middle, -near_far, other_cross) * flow_half
    )
    flow_near = jnp.where(in_near, flow_in, flow_out)
    flow_far = jnp.where(in_near, flow_out, flow_in)
    flow_core = join_core * (far_value_in + far_cross * flow_far - near_value_in - cross * flow_near)
    total_out = flow_near + push_out
    total_in = flow_core + push_in
    flux = jnp.concatenate(
        [jnp.where(upper_core, total_in, total_out), jnp.where(upper_core, total_out, total_in)], 0
    )

    chunks = 8
    return pl.pallas_call(
        functools.partial(finish_kernel, chunks),
        out_shape=jax.ShapeDtypeStruct((comps, rows, nx, nz), f32),
        in_specs=in_vmem(4),
        out_specs=hbm,
        scratch_shapes=[VMEM((comps, rows, nx, nz), f32), pltpu.SemaphoreType.DMA((chunks,))],
        compiler_params=params,
        name="finish",
    )(part, left, right, flux)


def solution(mesh):
    placed = (P(None, "wn", None, "xz"), P("wn", None, "xz"))
    return jax.shard_map(
        local, mesh=mesh, in_specs=placed, out_specs=P(None, "wn", None, "xz"), check_vma=False
    )
```

```python
import functools

import jax
import jax.numpy as jnp
from jax import lax
from jax.experimental import pallas as pl
from jax.experimental.pallas import tpu as pltpu
from jax.sharding import PartitionSpec as P

x_courant = 0.25
y_courant = 0.5
z_courant = 0.25
face_rate = 1000.0

SUB = 8
LANES = 128
VMEM = pltpu.VMEM
f32 = jnp.float32
bf16 = jnp.bfloat16


def lane_index():
    return lax.broadcasted_iota(jnp.int32, (SUB, LANES), 1)


def sub_index():
    return lax.broadcasted_iota(jnp.int32, (SUB, LANES), 0)


def tile(ref, *lead, t):
    return ref[(*lead, pl.ds(t * SUB, SUB), slice(None))]


def put(ref, value, *lead, t):
    ref[(*lead, pl.ds(t * SUB, SUB), slice(None))] = value


def square(ref, *lead, start, nx):
    rows = LANES // nx
    return ref[(*lead, pl.ds(start, rows))].reshape(LANES, LANES)


def shifted(ref, lead, t, tiles, forward, sub):
    if forward:
        if t < tiles - 1:
            return ref[(*lead, pl.ds(t * SUB + 1, SUB), slice(None))]
        mixed = jnp.where(sub == 0, tile(ref, *lead, t=0), tile(ref, *lead, t=t))
        return pltpu.roll(mixed, SUB - 1, 0)
    if t > 0:
        return ref[(*lead, pl.ds(t * SUB - 1, SUB), slice(None))]
    mixed = jnp.where(sub == SUB - 1, tile(ref, *lead, t=tiles - 1), tile(ref, *lead, t=t))
    return pltpu.roll(mixed, 1, 0)


def shifted(ref, lead, t, tiles, forward, sub):
    if forward:
        if t < tiles - 1:
            return ref[(*lead, pl.ds(t * SUB + 1, SUB), slice(None))]
        mixed = jnp.where(sub == 0, tile(ref, *lead, t=0), tile(ref, *lead, t=t))
        return pltpu.roll(mixed, SUB - 1, 0)
    if t > 0:
        return ref[(*lead, pl.ds(t * SUB - 1, SUB), slice(None))]
    mixed = jnp.where(sub == SUB - 1, tile(ref, *lead, t=tiles - 1), tile(ref, *lead, t=t))
    return pltpu.roll(mixed, 1, 0)


def head_kernel(
    chunk, early, count, vel_hbm, visc_hbm, place, vel, rhs, low, high, row_out, row_in, wid, hid, rec, fwd, flags, visc, sems, *bufs
):
    comps, rows, nx, _ = vel_hbm.shape
    tiles = nx // SUB
    group = LANES // nx
    chunks = rows // chunk
    sub = sub_index()

    def visc_copy(k):
        span = pl.ds(k * chunk, chunk)
        return pltpu.make_async_copy(visc_hbm.at[span], visc.at[span], sems.at[0, k])

    def vel_copy(k):
        span = pl.ds(k * chunk, chunk)
        inner = pl.ds(k * chunk + 1, chunk)
        return pltpu.make_async_copy(vel_hbm.at[:, span], vel.at[:, inner], sems.at[1, k])

    visc_copy(0).start()
    for k in range(chunks):
        vel_copy(k).start()
        if k < chunks - 1:
            visc_copy(k + 1).start()
    wn = place[0]
    core, chip = lax.rem(wn, 2), lax.div(wn, 2)
    marks = [core == 1, wn == 0, wn == count - 1, core != lax.rem(chip, 2), (chip == 1) | (chip == 2)]
    marks = [jnp.where(mark, 1.0, 0.0) for mark in marks]
    table, row = jnp.zeros((SUB, LANES), f32), sub_index()
    for k, mark in enumerate(marks):
        table = jnp.where(row == k, mark, table)
    flags[...] = table
    zero = jnp.zeros((SUB, LANES), f32)
    for c in range(comps):
        for t in range(tiles):
            put(vel, zero, c, 0, t=t)
            put(vel, zero, c, rows + 1, t=t)
    wall_low, wall_high = marks[1], marks[2]
    central = central_matrix()

    def arrive(g):
        for c in range(comps):
            turned = square(vel, c, start=g * group + 1, nx=nx).T
            low[c, pl.ds(g, 1), :] = turned[:1]
            high[c, pl.ds(g, 1), :] = turned[LANES - 1 :]

    def factor(start, state, last):
        state = list(state)
        for r in range(group):
            y = start + r
            end = last and r == group - 1
            for t in range(tiles):
                extra, cell, face, reach = state[4 * t : 4 * t + 4]
                inner = 1.0 + extra
                if end:
                    next_cell = cell
                    next_face = wall_high * (2.0 * cell)
                else:
                    next_cell = face_rate * tile(visc, y + 1, t=t)
                    next_face = cell + next_cell
                r_ = pltpu.reciprocal(inner + next_face, approx=False)
                w = r_ if end else next_face * r_
                h = face * r_
                reach = h * reach
                put(wid, w, y, t=t)
                put(hid, h, y, t=t)
                put(rec, r_, y, t=t)
                put(fwd, reach, y, t=t)
                state[4 * t : 4 * t + 4] = [w * inner, next_cell, next_face, reach]
        return tuple(state)

    several = chunk // group

    def body(k, state, sources, first=False, last=False):
        if not last:
            visc_copy(k + 1).wait()
        vel_copy(k).wait()
        for j in range(several):
            g = several * k + j
            arrive(g)
            state = factor(g * group, state, last and j == several - 1)
            if sources:
                if j or not first:
                    advect(vel, bufs[j - 1], rhs, g - 1)
                differ(vel, central, bufs[j], g, nx)
        return state

    visc_copy(0).wait()
    state = []
    one = jnp.ones((SUB, LANES), f32)
    for t in range(tiles):
        cell = face_rate * tile(visc, 0, t=t)
        state += [wall_low * (2.0 * cell), cell, one, one]
    split = early // several
    state = body(0, tuple(state), True, first=True)
    state = lax.fori_loop(1, split, lambda k, state: body(k, state, True), state)
    vel_copy(split).wait()
    advect(vel, bufs[-1], rhs, early - 1)

    def late(k, state):
        if_first = k > split

        @pl.when(if_first)
        def _():
            vel_copy(k).wait()

        visc_copy(k + 1).wait()
        for j in range(several):
            g = several * k + j
            arrive(g)
            state = factor(g * group, state, False)
        return state

    state = lax.fori_loop(split, chunks - 1, late, state)
    body(chunks - 1, state, False, last=True)

    upper = jnp.broadcast_to(marks[0], (SUB, LANES)) > 0.5
    for c in range(comps + 1):
        for t in range(tiles):
            if c < comps:
                first, end = tile(vel, c, 1, t=t), tile(vel, c, rows, t=t)
            else:
                first, end = tile(visc, 0, t=t), tile(visc, rows - 1, t=t)
            put(row_out, jnp.where(upper, end, first), c, t=t)
            put(row_in, jnp.where(upper, first, end), c, t=t)


def central_matrix():
    a = lax.broadcasted_iota(jnp.int32, (2 * LANES, LANES), 0) % LANES
    b = lax.broadcasted_iota(jnp.int32, (2 * LANES, LANES), 1)
    ahead = (a == (b + 1) % LANES).astype(f32)
    behind = (a == (b + LANES - 1) % LANES).astype(f32)
    return (z_courant * (ahead - behind)).astype(bf16)


def differ(vel, central, buf, g, nx):
    for c in range(buf.shape[0]):
        whole = square(vel, c, start=g * (LANES // nx) + 1, nx=nx)
        coarse = whole.astype(bf16)
        fine = (whole - coarse.astype(f32)).astype(bf16)
        buf[c] = jnp.dot(jnp.concatenate([coarse, fine], 1), central, preferred_element_type=f32)


def advect(vel, buf, rhs, g):
    comps, rows, nx, _ = rhs.shape
    tiles = nx // SUB
    group = LANES // nx
    sub = sub_index()
    for t in range(tiles):
        below = [tile(vel, c, g * group, t=t) for c in range(comps)]
        mid = [tile(vel, c, g * group + 1, t=t) for c in range(comps)]
        for r in range(group):
            y = g * group + r
            above = [tile(vel, c, y + 2, t=t) for c in range(comps)]
            rate_x, rate_y = x_courant * mid[0], y_courant * mid[1]
            for c in range(comps):
                lead = (c, y + 1)
                diff_x = shifted(vel, lead, t, tiles, True, sub) - shifted(vel, lead, t, tiles, False, sub)
                diff_y = above[c] - below[c]
                diff_z = buf[c, pl.ds(r * nx + t * SUB, SUB), :]
                put(rhs, mid[c] - (rate_x * diff_x + rate_y * diff_y + mid[2] * diff_z), c, y, t=t)
            below, mid = mid, above


def block_kernel(early, vel, rhs_in, wid, rec, fwd, rhs, left, right, ends, dots, edges, *bufs):
    comps, rows, nx, _ = rhs.shape
    tiles = nx // SUB
    group = LANES // nx
    groups = rows // group
    several = len(bufs)
    central = central_matrix()
    side = lax.broadcasted_iota(jnp.int32, (SUB, 2 * LANES), 0)
    spot = lax.broadcasted_iota(jnp.int32, (SUB, 2 * LANES), 1) % LANES
    ends_only = (((side == 0) & (spot == 0)) | ((side == 1) & (spot == LANES - 1))).astype(bf16)

    def process(g, state):
        state = list(state)
        for r in reversed(range(group)):
            y = g * group + r
            for t in range(tiles):
                ul, ur, *sums = state[8 * t : 8 * t + 8]
                w = tile(wid, y, t=t)
                ul, ur = tile(fwd, y, t=t) + w * ul, w * ur
                put(left, ul, y, t=t)
                put(right, ur, y, t=t)
                for c in range(comps):
                    source = tile(rhs, c, y, t=t)
                    sums[c] = sums[c] + ul * source
                    sums[comps + c] = sums[comps + c] + ur * source
                state[8 * t : 8 * t + 8] = [ul, ur, *sums]
        return tuple(state)

    def pack(g):
        turned = square(left, start=g * group, nx=nx).T
        edges[0, pl.ds(g, 1), :] = turned[:1]
        edges[1, pl.ds(g, 1), :] = turned[LANES - 1 :]
        whole = square(right, start=g * group, nx=nx)
        coarse = whole.astype(bf16)
        fine = (whole - coarse.astype(f32)).astype(bf16)
        picked = lax.dot_general(
            ends_only, jnp.concatenate([coarse, fine], 1), (((1,), (1,)), ((), ())), preferred_element_type=f32
        )
        edges[2, pl.ds(g, 1), :] = picked[:1]
        edges[3, pl.ds(g, 1), :] = picked[1:2]

    def fresh(m, state):
        first = groups - 1 - several * m
        for j in range(several + 1):
            g = first - j
            if j < several:
                differ(vel, central, bufs[j], g, nx)
            if j:
                advect(vel, bufs[j - 1], rhs, g + 1)
                state = process(g + 1, state)
                pack(g + 1)
        return state

    def body(m, state):
        first = early - 1 - several * m
        for j in range(several):
            state = process(first - j, state)
            pack(first - j)
        return state

    zero, one = jnp.zeros((SUB, LANES), f32), jnp.ones((SUB, LANES), f32)
    state = ([zero, one] + [zero] * 6) * tiles
    state = lax.fori_loop(0, (groups - early) // several, fresh, tuple(state))
    state = lax.fori_loop(0, early // several, body, state)
    for t in range(tiles):
        ul, ur, *sums = state[8 * t : 8 * t + 8]
        put(ends, ul, 0, t=t)
        put(ends, tile(fwd, rows - 1, t=t), 1, t=t)
        put(ends, tile(rec, rows - 1, t=t), 2, t=t)
        for k in range(6):
            put(dots, sums[k], k, t=t)


def edge_kernel(low, high, from_left, from_right, edges, dots, edge_low, edge_high, values):
    comps, groups, _ = low.shape
    _, nx, _ = dots.shape
    lane, sub = lane_index(), sub_index()
    edge_low[...] = z_courant * low[2] * (from_left[...] - high[...])
    edge_high[...] = -z_courant * high[2] * (from_right[...] - low[...])
    for k in range(2):
        for c in range(comps):
            line_low = jnp.sum(edges[2 * k] * edge_low[c], 0, keepdims=True)
            line_high = jnp.sum(edges[2 * k + 1] * edge_high[c], 0, keepdims=True)
            for t in range(nx // SUB):
                mine = lane % nx == sub + t * SUB
                at_low = jnp.sum(jnp.where(mine, line_low, 0.0), 1, keepdims=True)
                at_high = jnp.sum(jnp.where(mine, line_high, 0.0), 1, keepdims=True)
                add = jnp.where(lane == 0, at_low, jnp.where(lane == LANES - 1, at_high, 0.0))
                put(values, tile(dots, comps * k + c, t=t) + add, comps * k + c, t=t)


def sweep_kernel(rhs, low, high, wid, hid, rec, face, out, face_out, buf_a, buf_b):
    comps, rows, nx, _ = rhs.shape
    tiles = nx // SUB
    group = LANES // nx
    groups = rows // group
    sub = sub_index()
    zero = jnp.zeros((SUB, LANES), f32)
    middle = jnp.zeros((LANES - 2 * SUB, LANES), f32)
    face_out[...] = face[...]

    def spread(buf, g):
        for c in range(comps):
            top = jnp.where(sub == 0, low[c, pl.ds(g, 1), :], 0.0)
            bottom = jnp.where(sub == SUB - 1, high[c, pl.ds(g, 1), :], 0.0)
            buf[c] = jnp.concatenate([top, middle, bottom], 0).T

    def process(g, buf, state):
        new = list(state)
        for r in range(group):
            y = g * group + r
            for t in range(tiles):
                r_, h = tile(rec, y, t=t), tile(hid, y, t=t)
                for c in range(comps):
                    k = t * comps + c
                    source = tile(rhs, c, y, t=t) + buf[c, pl.ds(r * nx + t * SUB, SUB), :]
                    new[k] = source * r_ + h * new[k]
                    put(out, new[k], c, y, t=t)
        return tuple(new)

    def forward(m, state):
        g = 2 * m
        spread(buf_b, g + 1)
        state = process(g, buf_a, state)
        spread(buf_a, jnp.minimum(g + 2, groups - 1))
        return process(g + 1, buf_b, state)

    spread(buf_a, 0)
    lax.fori_loop(0, groups // 2, forward, (zero,) * (comps * tiles))

    def backward(k, state):
        y = rows - 1 - k
        new = list(state)
        for t in range(tiles):
            w = tile(wid, y, t=t)
            for c in range(comps):
                k = t * comps + c
                new[k] = tile(out, c, y, t=t) + w * state[k]
                put(out, new[k], c, y, t=t)
        return tuple(new)

    lax.fori_loop(0, rows, backward, (zero,) * (comps * tiles), unroll=4)


def finish_kernel(chunks, part, left, right, flux, out_hbm, out, sems):
    comps, rows, nx, _ = part.shape
    tiles = nx // SUB
    step = rows // chunks

    copies = []
    for k in range(chunks):
        for t in range(tiles):
            fl = [tile(flux, c, t=t) for c in range(comps)]
            fr = [tile(flux, comps + c, t=t) for c in range(comps)]

            def row(y, carry):
                ul, ur = tile(left, y, t=t), tile(right, y, t=t)
                for c in range(comps):
                    put(out, tile(part, c, y, t=t) + (ul * fl[c] + ur * fr[c]), c, y, t=t)
                return carry

            lax.fori_loop(k * step, (k + 1) * step, row, 0, unroll=4)
        span = pl.ds(k * step, step)
        copies.append(pltpu.make_async_copy(out.at[:, span], out_hbm.at[:, span], sems.at[k]))
        copies[-1].start()
    for copy in copies:
        copy.wait()


def vmem_out(*shape):
    return VMEM(shape, f32)


def in_vmem(n):
    return [pl.BlockSpec(memory_space=VMEM)] * n


def cost(flops, moved):
    return pl.CostEstimate(flops=flops, bytes_accessed=moved, transcendentals=0)


def local(velocity, viscosity):
    comps, rows, nx, nz = velocity.shape
    cells = rows * nx * nz
    groups = rows * nx // LANES
    hbm = pl.BlockSpec(memory_space=pltpu.HBM)
    params = pltpu.CompilerParams(vmem_limit_bytes=8 * 2**20)

    wn = lax.axis_index("wn")
    count = lax.axis_size("wn")
    planes = lax.axis_size("xz")
    chunk = 4 * LANES // nx
    early = 8
    vel, rhs, low, high, row_out, row_in, wid, hid, rec, fwd, flags = pl.pallas_call(
        functools.partial(head_kernel, chunk, early, count),
        out_shape=(
            vmem_out(comps, rows + 2, nx, nz),
            vmem_out(comps, rows, nx, nz),
            vmem_out(comps, groups, LANES),
            vmem_out(comps, groups, LANES),
            vmem_out(comps + 1, nx, nz),
            vmem_out(comps + 1, nx, nz),
            vmem_out(rows, nx, nz),
            vmem_out(rows, nx, nz),
            vmem_out(rows, nx, nz),
            vmem_out(rows, nx, nz),
            vmem_out(SUB, LANES),
        ),
        in_specs=[hbm, hbm, pl.BlockSpec(memory_space=pltpu.SMEM)],
        out_specs=in_vmem(11),
        scratch_shapes=[
            VMEM((rows, nx, nz), f32),
            pltpu.SemaphoreType.DMA((2, rows // chunk)),
            *[VMEM((comps, LANES, LANES), f32)] * (chunk * nx // LANES),
        ],
        compiler_params=pltpu.CompilerParams(vmem_limit_bytes=39 * 2**20),
        name="head",
    )(velocity, viscosity, wn.astype(jnp.int32).reshape(1))

    with jax.named_scope("halo_z"):
        from_left = lax.ppermute(high, "xz", [(i, (i + 1) % planes) for i in range(planes)])
        from_right = lax.ppermute(low, "xz", [((i + 1) % planes, i) for i in range(planes)])
    with jax.named_scope("halo_y"):
        pairs = [(i, (i + 1) % count if i % 2 else (i - 1) % count) for i in range(count)]
        row_other = lax.ppermute(row_out, "wn", pairs)

    rhs, left, right, ends, dots, edges = pl.pallas_call(
        functools.partial(block_kernel, early),
        out_shape=(
            vmem_out(comps, rows, nx, nz),
            vmem_out(rows, nx, nz),
            vmem_out(rows, nx, nz),
            vmem_out(3, nx, nz),
            vmem_out(2 * comps, nx, nz),
            vmem_out(4, groups, LANES),
        ),
        in_specs=in_vmem(5),
        out_specs=in_vmem(6),
        scratch_shapes=[VMEM((comps, LANES, LANES), f32)] * 8,
        input_output_aliases={1: 0},
        compiler_params=params,
        cost_estimate=cost(40 * cells, 32 * cells),
        name="block",
    )(vel, rhs, wid, rec, fwd)

    edge_low, edge_high, values = pl.pallas_call(
        edge_kernel,
        out_shape=(
            vmem_out(comps, groups, LANES),
            vmem_out(comps, groups, LANES),
            vmem_out(2 * comps, nx, nz),
        ),
        in_specs=in_vmem(6),
        out_specs=in_vmem(3),
        compiler_params=params,
        name="edge",
    )(low, high, from_left, from_right, edges, dots)

    upper_core, first_block, last_block, in_near, middle = (flags[k : k + 1] > 0.5 for k in range(5))
    value_first, value_last = values[:comps], values[comps:]

    cross = ends[1]
    own_out = jnp.where(upper_core, ends[2], ends[0])
    own_in = jnp.where(upper_core, ends[0], ends[2])
    value_out = jnp.where(upper_core, value_last, value_first)
    value_in = jnp.where(upper_core, value_first, value_last)
    sign_in = jnp.where(upper_core, y_courant, -y_courant)
    push_out = jnp.where(first_block | last_block, 0.0, -sign_in * row_out[1] * row_other[:comps])
    face_out = face_rate * (row_out[3] + row_other[3])
    value_out = value_out + own_out * push_out
    value_in = value_in + cross * push_out

    send = jnp.concatenate(
        [jnp.stack([own_out, cross, own_in]), value_out, value_in, row_in, face_out[None]], 0
    )
    with jax.named_scope("exchange_core"):
        got = lax.ppermute(send, "wn", [(i, i ^ 1) for i in range(count)])
    far_out, far_cross, far_in = got[0], got[1], got[2]
    far_value_out, far_value_in = got[3:6], got[6:9]
    far_row, far_face = got[9:13], got[13]
    push_in = sign_in * row_in[1] * far_row[:comps]
    far_push = -sign_in * far_row[1] * row_in[:comps]
    near_value_in = value_in + own_in * push_in
    near_value_out = value_out + cross * push_in
    far_value_out = far_value_out + far_cross * far_push
    far_value_in = far_value_in + far_in * far_push
    join_core = 1.0 / (1.0 / (face_rate * (row_in[3] + far_row[3])) + own_in + far_in)
    flow = join_core * (far_value_in - near_value_in)
    near_near = own_out - cross * cross * join_core
    near_far = cross * far_cross * join_core
    far_far = far_out - far_cross * far_cross * join_core
    near_value = near_value_out + cross * flow
    far_value = far_value_out - far_cross * flow

    chip_in = jnp.where(in_near, near_near, far_far)
    chip_out = jnp.where(in_near, far_far, near_near)
    chip_value_in = jnp.where(in_near, near_value, far_value)
    chip_value_out = jnp.where(in_near, far_value, near_value)
    chip_face_in = jnp.where(in_near, face_out, far_face)
    chip_face_out = jnp.where(in_near, far_face, face_out)
    send = jnp.concatenate(
        [jnp.stack([chip_out, near_far, chip_in, chip_face_out]), chip_value_out, chip_value_in], 0
    )
    with jax.named_scope("exchange_chip"):
        got = lax.ppermute(send, "wn", [(i, i ^ 2) for i in range(count)])

    part, chip_face_in = pl.pallas_call(
        sweep_kernel,
        out_shape=(vmem_out(comps, rows, nx, nz), vmem_out(nx, nz)),
        in_specs=in_vmem(7),
        out_specs=in_vmem(2),
        scratch_shapes=[VMEM((comps, LANES, LANES), f32)] * 2,
        compiler_params=params,
        cost_estimate=cost(30 * cells, 30 * cells),
        name="sweep",
    )(rhs, edge_low, edge_high, wid, hid, rec, chip_face_in)

    other_out, other_cross, other_in, other_face = got[0], got[1], got[2], got[3]
    other_value_out, other_value_in = got[4:7], got[7:10]
    join_chip = 1.0 / (1.0 / chip_face_in + chip_in + other_in)
    flow = join_chip * (other_value_in - chip_value_in)
    half_own = jnp.where(
        middle, chip_out - near_far * near_far * join_chip, other_out - other_cross * other_cross * join_chip
    )
    half_value = jnp.where(middle, chip_value_out + near_far * flow, other_value_out - other_cross * flow)
    half_face = jnp.where(middle, chip_face_out, other_face)
    send = jnp.concatenate([half_own[None], half_value], 0)
    with jax.named_scope("exchange_half"):
        got = lax.ppermute(send, "wn", [(i, i ^ 6) for i in range(count)])
    flow_half = (got[1:] - half_value) / (1.0 / half_face + half_own + got[0])

    flow_out = jnp.where(middle, flow_half, 0.0)
    flow_in = join_chip * (
        other_value_in
        - chip_value_in
        + jnp.where(middle, -near_far, other_cross) * flow_half
    )
    flow_near = jnp.where(in_near, flow_in, flow_out)
    flow_far = jnp.where(in_near, flow_out, flow_in)
    flow_core = join_core * (far_value_in + far_cross * flow_far - near_value_in - cross * flow_near)
    total_out = flow_near + push_out
    total_in = flow_core + push_in
    flux = jnp.concatenate(
        [jnp.where(upper_core, total_in, total_out), jnp.where(upper_core, total_out, total_in)], 0
    )

    chunks = 8
    return pl.pallas_call(
        functools.partial(finish_kernel, chunks),
        out_shape=jax.ShapeDtypeStruct((comps, rows, nx, nz), f32),
        in_specs=in_vmem(4),
        out_specs=hbm,
        scratch_shapes=[VMEM((comps, rows, nx, nz), f32), pltpu.SemaphoreType.DMA((chunks,))],
        compiler_params=params,
        name="finish",
    )(part, left, right, flux)


def solution(mesh):
    placed = (P(None, "wn", None, "xz"), P("wn", None, "xz"))
    return jax.shard_map(
        local, mesh=mesh, in_specs=placed, out_specs=P(None, "wn", None, "xz"), check_vma=False
    )
```

```python
import functools

import jax
import jax.numpy as jnp
from jax import lax
from jax.experimental import pallas as pl
from jax.experimental.pallas import tpu as pltpu
from jax.sharding import PartitionSpec as P

x_courant = 0.25
y_courant = 0.5
z_courant = 0.25
face_rate = 1000.0

SUB = 8
LANES = 128
VMEM = pltpu.VMEM
f32 = jnp.float32
bf16 = jnp.bfloat16


def lane_index():
    return lax.broadcasted_iota(jnp.int32, (SUB, LANES), 1)


def sub_index():
    return lax.broadcasted_iota(jnp.int32, (SUB, LANES), 0)


def tile(ref, *lead, t):
    return ref[(*lead, pl.ds(t * SUB, SUB), slice(None))]


def put(ref, value, *lead, t):
    ref[(*lead, pl.ds(t * SUB, SUB), slice(None))] = value


def square(ref, *lead, start, nx):
    rows = LANES // nx
    return ref[(*lead, pl.ds(start, rows))].reshape(LANES, LANES)


def shifted(ref, lead, t, tiles, forward, sub):
    if forward:
        if t < tiles - 1:
            return ref[(*lead, pl.ds(t * SUB + 1, SUB), slice(None))]
        mixed = jnp.where(sub == 0, tile(ref, *lead, t=0), tile(ref, *lead, t=t))
        return pltpu.roll(mixed, SUB - 1, 0)
    if t > 0:
        return ref[(*lead, pl.ds(t * SUB - 1, SUB), slice(None))]
    mixed = jnp.where(sub == SUB - 1, tile(ref, *lead, t=tiles - 1), tile(ref, *lead, t=t))
    return pltpu.roll(mixed, 1, 0)


def shifted(ref, lead, t, tiles, forward, sub):
    if forward:
        if t < tiles - 1:
            return ref[(*lead, pl.ds(t * SUB + 1, SUB), slice(None))]
        mixed = jnp.where(sub == 0, tile(ref, *lead, t=0), tile(ref, *lead, t=t))
        return pltpu.roll(mixed, SUB - 1, 0)
    if t > 0:
        return ref[(*lead, pl.ds(t * SUB - 1, SUB), slice(None))]
    mixed = jnp.where(sub == SUB - 1, tile(ref, *lead, t=tiles - 1), tile(ref, *lead, t=t))
    return pltpu.roll(mixed, 1, 0)


def head_kernel(
    chunk, early, count, vel_hbm, visc_hbm, place, vel, rhs, low, high, row_out, row_in, wid, hid, rec, fwd, flags, visc, sems, *bufs
):
    comps, rows, nx, _ = vel_hbm.shape
    tiles = nx // SUB
    group = LANES // nx
    chunks = rows // chunk
    sub = sub_index()

    def visc_copy(k):
        span = pl.ds(k * chunk, chunk)
        return pltpu.make_async_copy(visc_hbm.at[span], visc.at[span], sems.at[0, k])

    def vel_copy(k):
        span = pl.ds(k * chunk, chunk)
        inner = pl.ds(k * chunk + 1, chunk)
        return pltpu.make_async_copy(vel_hbm.at[:, span], vel.at[:, inner], sems.at[1, k])

    visc_copy(0).start()
    for k in range(chunks):
        vel_copy(k).start()
        if k < chunks - 1:
            visc_copy(k + 1).start()
    wn = place[0]
    core, chip = lax.rem(wn, 2), lax.div(wn, 2)
    marks = [core == 1, wn == 0, wn == count - 1, lax.rem(chip, 2) == 1, chip >= 2]
    marks = [jnp.where(mark, 1.0, 0.0) for mark in marks]
    table, row = jnp.zeros((SUB, LANES), f32), sub_index()
    for k, mark in enumerate(marks):
        table = jnp.where(row == k, mark, table)
    flags[...] = table
    zero = jnp.zeros((SUB, LANES), f32)
    for c in range(comps):
        for t in range(tiles):
            put(vel, zero, c, 0, t=t)
            put(vel, zero, c, rows + 1, t=t)
    wall_low, wall_high = marks[1], marks[2]
    central = central_matrix()

    def arrive(g):
        for c in range(comps):
            turned = square(vel, c, start=g * group + 1, nx=nx).T
            low[c, pl.ds(g, 1), :] = turned[:1]
            high[c, pl.ds(g, 1), :] = turned[LANES - 1 :]

    def factor(start, state, last):
        state = list(state)
        for r in range(group):
            y = start + r
            end = last and r == group - 1
            for t in range(tiles):
                extra, cell, face, reach = state[4 * t : 4 * t + 4]
                inner = 1.0 + extra
                if end:
                    next_cell = cell
                    next_face = wall_high * (2.0 * cell)
                else:
                    next_cell = face_rate * tile(visc, y + 1, t=t)
                    next_face = cell + next_cell
                r_ = pltpu.reciprocal(inner + next_face, approx=False)
                w = r_ if end else next_face * r_
                h = face * r_
                reach = h * reach
                put(wid, w, y, t=t)
                put(hid, h, y, t=t)
                put(rec, r_, y, t=t)
                put(fwd, reach, y, t=t)
                state[4 * t : 4 * t + 4] = [w * inner, next_cell, next_face, reach]
        return tuple(state)

    several = chunk // group

    def body(k, state, sources, first=False, last=False):
        if not last:
            visc_copy(k + 1).wait()
        vel_copy(k).wait()
        for j in range(several):
            g = several * k + j
            arrive(g)
            state = factor(g * group, state, last and j == several - 1)
            if sources:
                if j or not first:
                    advect(vel, bufs[j - 1], rhs, g - 1)
                differ(vel, central, bufs[j], g, nx)
        return state

    visc_copy(0).wait()
    state = []
    one = jnp.ones((SUB, LANES), f32)
    for t in range(tiles):
        cell = face_rate * tile(visc, 0, t=t)
        state += [wall_low * (2.0 * cell), cell, one, one]
    split = early // several
    state = body(0, tuple(state), True, first=True)
    state = lax.fori_loop(1, split, lambda k, state: body(k, state, True), state)
    vel_copy(split).wait()
    advect(vel, bufs[-1], rhs, early - 1)

    def late(k, state):
        if_first = k > split

        @pl.when(if_first)
        def _():
            vel_copy(k).wait()

        visc_copy(k + 1).wait()
        for j in range(several):
            g = several * k + j
            arrive(g)
            state = factor(g * group, state, False)
        return state

    state = lax.fori_loop(split, chunks - 1, late, state)
    body(chunks - 1, state, False, last=True)

    upper = jnp.broadcast_to(marks[0], (SUB, LANES)) > 0.5
    for c in range(comps + 1):
        for t in range(tiles):
            if c < comps:
                first, end = tile(vel, c, 1, t=t), tile(vel, c, rows, t=t)
            else:
                first, end = tile(visc, 0, t=t), tile(visc, rows - 1, t=t)
            put(row_out, jnp.where(upper, end, first), c, t=t)
            put(row_in, jnp.where(upper, first, end), c, t=t)


def central_matrix():
    a = lax.broadcasted_iota(jnp.int32, (2 * LANES, LANES), 0) % LANES
    b = lax.broadcasted_iota(jnp.int32, (2 * LANES, LANES), 1)
    ahead = (a == (b + 1) % LANES).astype(f32)
    behind = (a == (b + LANES - 1) % LANES).astype(f32)
    return (z_courant * (ahead - behind)).astype(bf16)


def differ(vel, central, buf, g, nx):
    for c in range(buf.shape[0]):
        whole = square(vel, c, start=g * (LANES // nx) + 1, nx=nx)
        coarse = whole.astype(bf16)
        fine = (whole - coarse.astype(f32)).astype(bf16)
        buf[c] = jnp.dot(jnp.concatenate([coarse, fine], 1), central, preferred_element_type=f32)


def advect(vel, buf, rhs, g):
    comps, rows, nx, _ = rhs.shape
    tiles = nx // SUB
    group = LANES // nx
    sub = sub_index()
    for t in range(tiles):
        below = [tile(vel, c, g * group, t=t) for c in range(comps)]
        mid = [tile(vel, c, g * group + 1, t=t) for c in range(comps)]
        for r in range(group):
            y = g * group + r
            above = [tile(vel, c, y + 2, t=t) for c in range(comps)]
            rate_x, rate_y = x_courant * mid[0], y_courant * mid[1]
            for c in range(comps):
                lead = (c, y + 1)
                diff_x = shifted(vel, lead, t, tiles, True, sub) - shifted(vel, lead, t, tiles, False, sub)
                diff_y = above[c] - below[c]
                diff_z = buf[c, pl.ds(r * nx + t * SUB, SUB), :]
                put(rhs, mid[c] - (rate_x * diff_x + rate_y * diff_y + mid[2] * diff_z), c, y, t=t)
            below, mid = mid, above


def block_kernel(early, vel, rhs_in, wid, rec, fwd, rhs, left, right, ends, dots, edges, *bufs):
    comps, rows, nx, _ = rhs.shape
    tiles = nx // SUB
    group = LANES // nx
    groups = rows // group
    several = len(bufs)
    central = central_matrix()
    side = lax.broadcasted_iota(jnp.int32, (SUB, 2 * LANES), 0)
    spot = lax.broadcasted_iota(jnp.int32, (SUB, 2 * LANES), 1) % LANES
    ends_only = (((side == 0) & (spot == 0)) | ((side == 1) & (spot == LANES - 1))).astype(bf16)

    def process(g, state):
        state = list(state)
        for r in reversed(range(group)):
            y = g * group + r
            for t in range(tiles):
                ul, ur, *sums = state[8 * t : 8 * t + 8]
                w = tile(wid, y, t=t)
                ul, ur = tile(fwd, y, t=t) + w * ul, w * ur
                put(left, ul, y, t=t)
                put(right, ur, y, t=t)
                for c in range(comps):
                    source = tile(rhs, c, y, t=t)
                    sums[c] = sums[c] + ul * source
                    sums[comps + c] = sums[comps + c] + ur * source
                state[8 * t : 8 * t + 8] = [ul, ur, *sums]
        return tuple(state)

    def pack(g):
        turned = square(left, start=g * group, nx=nx).T
        edges[0, pl.ds(g, 1), :] = turned[:1]
        edges[1, pl.ds(g, 1), :] = turned[LANES - 1 :]
        whole = square(right, start=g * group, nx=nx)
        coarse = whole.astype(bf16)
        fine = (whole - coarse.astype(f32)).astype(bf16)
        picked = lax.dot_general(
            ends_only, jnp.concatenate([coarse, fine], 1), (((1,), (1,)), ((), ())), preferred_element_type=f32
        )
        edges[2, pl.ds(g, 1), :] = picked[:1]
        edges[3, pl.ds(g, 1), :] = picked[1:2]

    def fresh(m, state):
        first = groups - 1 - several * m
        for j in range(several + 1):
            g = first - j
            if j < several:
                differ(vel, central, bufs[j], g, nx)
            if j:
                advect(vel, bufs[j - 1], rhs, g + 1)
                state = process(g + 1, state)
                pack(g + 1)
        return state

    def body(m, state):
        first = early - 1 - several * m
        for j in range(several):
            state = process(first - j, state)
            pack(first - j)
        return state

    zero, one = jnp.zeros((SUB, LANES), f32), jnp.ones((SUB, LANES), f32)
    state = ([zero, one] + [zero] * 6) * tiles
    state = lax.fori_loop(0, (groups - early) // several, fresh, tuple(state))
    state = lax.fori_loop(0, early // several, body, state)
    for t in range(tiles):
        ul, ur, *sums = state[8 * t : 8 * t + 8]
        put(ends, ul, 0, t=t)
        put(ends, tile(fwd, rows - 1, t=t), 1, t=t)
        put(ends, tile(rec, rows - 1, t=t), 2, t=t)
        for k in range(6):
            put(dots, sums[k], k, t=t)


def edge_kernel(low, high, from_left, from_right, edges, dots, edge_low, edge_high, values):
    comps, groups, _ = low.shape
    _, nx, _ = dots.shape
    lane, sub = lane_index(), sub_index()
    edge_low[...] = z_courant * low[2] * (from_left[...] - high[...])
    edge_high[...] = -z_courant * high[2] * (from_right[...] - low[...])
    for k in range(2):
        for c in range(comps):
            line_low = jnp.sum(edges[2 * k] * edge_low[c], 0, keepdims=True)
            line_high = jnp.sum(edges[2 * k + 1] * edge_high[c], 0, keepdims=True)
            for t in range(nx // SUB):
                mine = lane % nx == sub + t * SUB
                at_low = jnp.sum(jnp.where(mine, line_low, 0.0), 1, keepdims=True)
                at_high = jnp.sum(jnp.where(mine, line_high, 0.0), 1, keepdims=True)
                add = jnp.where(lane == 0, at_low, jnp.where(lane == LANES - 1, at_high, 0.0))
                put(values, tile(dots, comps * k + c, t=t) + add, comps * k + c, t=t)


def sweep_kernel(rhs, low, high, wid, hid, rec, face, out, face_out, buf_a, buf_b):
    comps, rows, nx, _ = rhs.shape
    tiles = nx // SUB
    group = LANES // nx
    groups = rows // group
    sub = sub_index()
    zero = jnp.zeros((SUB, LANES), f32)
    middle = jnp.zeros((LANES - 2 * SUB, LANES), f32)
    face_out[...] = face[...]

    def spread(buf, g):
        for c in range(comps):
            top = jnp.where(sub == 0, low[c, pl.ds(g, 1), :], 0.0)
            bottom = jnp.where(sub == SUB - 1, high[c, pl.ds(g, 1), :], 0.0)
            buf[c] = jnp.concatenate([top, middle, bottom], 0).T

    def process(g, buf, state):
        new = list(state)
        for r in range(group):
            y = g * group + r
            for t in range(tiles):
                r_, h = tile(rec, y, t=t), tile(hid, y, t=t)
                for c in range(comps):
                    k = t * comps + c
                    source = tile(rhs, c, y, t=t) + buf[c, pl.ds(r * nx + t * SUB, SUB), :]
                    new[k] = source * r_ + h * new[k]
                    put(out, new[k], c, y, t=t)
        return tuple(new)

    def forward(m, state):
        g = 2 * m
        spread(buf_b, g + 1)
        state = process(g, buf_a, state)
        spread(buf_a, jnp.minimum(g + 2, groups - 1))
        return process(g + 1, buf_b, state)

    spread(buf_a, 0)
    lax.fori_loop(0, groups // 2, forward, (zero,) * (comps * tiles))

    def backward(k, state):
        y = rows - 1 - k
        new = list(state)
        for t in range(tiles):
            w = tile(wid, y, t=t)
            for c in range(comps):
                k = t * comps + c
                new[k] = tile(out, c, y, t=t) + w * state[k]
                put(out, new[k], c, y, t=t)
        return tuple(new)

    lax.fori_loop(0, rows, backward, (zero,) * (comps * tiles), unroll=4)


def finish_kernel(chunks, part, left, right, flux, out_hbm, out, sems):
    comps, rows, nx, _ = part.shape
    tiles = nx // SUB
    step = rows // chunks

    copies = []
    for k in range(chunks):
        for t in range(tiles):
            fl = [tile(flux, c, t=t) for c in range(comps)]
            fr = [tile(flux, comps + c, t=t) for c in range(comps)]

            def row(y, carry):
                ul, ur = tile(left, y, t=t), tile(right, y, t=t)
                for c in range(comps):
                    put(out, tile(part, c, y, t=t) + (ul * fl[c] + ur * fr[c]), c, y, t=t)
                return carry

            lax.fori_loop(k * step, (k + 1) * step, row, 0, unroll=4)
        span = pl.ds(k * step, step)
        copies.append(pltpu.make_async_copy(out.at[:, span], out_hbm.at[:, span], sems.at[k]))
        copies[-1].start()
    for copy in copies:
        copy.wait()


def vmem_out(*shape):
    return VMEM(shape, f32)


def in_vmem(n):
    return [pl.BlockSpec(memory_space=VMEM)] * n


def cost(flops, moved):
    return pl.CostEstimate(flops=flops, bytes_accessed=moved, transcendentals=0)


def local(velocity, viscosity):
    comps, rows, nx, nz = velocity.shape
    cells = rows * nx * nz
    groups = rows * nx // LANES
    hbm = pl.BlockSpec(memory_space=pltpu.HBM)
    params = pltpu.CompilerParams(vmem_limit_bytes=8 * 2**20)

    wn = lax.axis_index("wn")
    count = lax.axis_size("wn")
    planes = lax.axis_size("xz")
    chunk = 4 * LANES // nx
    early = 8
    vel, rhs, low, high, row_out, row_in, wid, hid, rec, fwd, flags = pl.pallas_call(
        functools.partial(head_kernel, chunk, early, count),
        out_shape=(
            vmem_out(comps, rows + 2, nx, nz),
            vmem_out(comps, rows, nx, nz),
            vmem_out(comps, groups, LANES),
            vmem_out(comps, groups, LANES),
            vmem_out(comps + 1, nx, nz),
            vmem_out(comps + 1, nx, nz),
            vmem_out(rows, nx, nz),
            vmem_out(rows, nx, nz),
            vmem_out(rows, nx, nz),
            vmem_out(rows, nx, nz),
            vmem_out(SUB, LANES),
        ),
        in_specs=[hbm, hbm, pl.BlockSpec(memory_space=pltpu.SMEM)],
        out_specs=in_vmem(11),
        scratch_shapes=[
            VMEM((rows, nx, nz), f32),
            pltpu.SemaphoreType.DMA((2, rows // chunk)),
            *[VMEM((comps, LANES, LANES), f32)] * (chunk * nx // LANES),
        ],
        compiler_params=pltpu.CompilerParams(vmem_limit_bytes=39 * 2**20),
        name="head",
    )(velocity, viscosity, wn.astype(jnp.int32).reshape(1))

    with jax.named_scope("halo_z"):
        from_left = lax.ppermute(high, "xz", [(i, (i + 1) % planes) for i in range(planes)])
        from_right = lax.ppermute(low, "xz", [((i + 1) % planes, i) for i in range(planes)])
    with jax.named_scope("halo_y"):
        pairs = [(i, (i + 1) % count if i % 2 else (i - 1) % count) for i in range(count)]
        row_other = lax.ppermute(row_out, "wn", pairs)

    rhs, left, right, ends, dots, edges = pl.pallas_call(
        functools.partial(block_kernel, early),
        out_shape=(
            vmem_out(comps, rows, nx, nz),
            vmem_out(rows, nx, nz),
            vmem_out(rows, nx, nz),
            vmem_out(3, nx, nz),
            vmem_out(2 * comps, nx, nz),
            vmem_out(4, groups, LANES),
        ),
        in_specs=in_vmem(5),
        out_specs=in_vmem(6),
        scratch_shapes=[VMEM((comps, LANES, LANES), f32)] * 8,
        input_output_aliases={1: 0},
        compiler_params=params,
        cost_estimate=cost(40 * cells, 32 * cells),
        name="block",
    )(vel, rhs, wid, rec, fwd)

    edge_low, edge_high, values = pl.pallas_call(
        edge_kernel,
        out_shape=(
            vmem_out(comps, groups, LANES),
            vmem_out(comps, groups, LANES),
            vmem_out(2 * comps, nx, nz),
        ),
        in_specs=in_vmem(6),
        out_specs=in_vmem(3),
        compiler_params=params,
        name="edge",
    )(low, high, from_left, from_right, edges, dots)

    upper_core, first_block, last_block, odd_chip, high_chip = (flags[k : k + 1] > 0.5 for k in range(5))
    value_first, value_last = values[:comps], values[comps:]

    cross = ends[1]
    own_out = jnp.where(upper_core, ends[2], ends[0])
    own_in = jnp.where(upper_core, ends[0], ends[2])
    value_out = jnp.where(upper_core, value_last, value_first)
    value_in = jnp.where(upper_core, value_first, value_last)
    sign_in = jnp.where(upper_core, y_courant, -y_courant)
    push_out = jnp.where(first_block | last_block, 0.0, -sign_in * row_out[1] * row_other[:comps])
    face_out = face_rate * (row_out[3] + row_other[3])
    value_out = value_out + own_out * push_out
    value_in = value_in + cross * push_out

    def mine(part):
        return jnp.where(upper_core, part[..., nx // 2 :, :], part[..., : nx // 2, :])

    def others(part):
        return jnp.where(upper_core, part[..., : nx // 2, :], part[..., nx // 2 :, :])

    parts = [own_out[None], cross[None], own_in[None], value_out, value_in, row_in, face_out[None]]
    send = jnp.concatenate([others(part) for part in parts], 0)
    with jax.named_scope("exchange_core"):
        got = lax.ppermute(send, "wn", [(i, i ^ 1) for i in range(count)])
    far_out, far_cross, far_in = got[0], got[1], got[2]
    far_value_out, far_value_in = got[3:6], got[6:9]
    far_row, far_face = got[9:13], got[13]
    own_out, cross, own_in, value_out, value_in, near_row, near_face = map(
        mine, (own_out, cross, own_in, value_out, value_in, row_in, face_out)
    )
    push_in = sign_in * near_row[1] * far_row[:comps]
    far_push = -sign_in * far_row[1] * near_row[:comps]
    near_value_in = value_in + own_in * push_in
    near_value_out = value_out + cross * push_in
    far_value_out = far_value_out + far_cross * far_push
    far_value_in = far_value_in + far_in * far_push
    join_core = 1.0 / (1.0 / (face_rate * (near_row[3] + far_row[3])) + own_in + far_in)
    flow = join_core * (far_value_in - near_value_in)
    near_near = own_out - cross * cross * join_core
    far_far = far_out - far_cross * far_cross * join_core
    near_value = near_value_out + cross * flow
    far_value = far_value_out - far_cross * flow

    face_low = jnp.where(upper_core, far_face, near_face)
    send = jnp.concatenate(
        [
            jnp.where(upper_core, far_far, near_near)[None],
            (cross * far_cross * join_core)[None],
            jnp.where(upper_core, near_near, far_far)[None],
            face_low[None],
            jnp.where(upper_core, far_value, near_value),
            jnp.where(upper_core, near_value, far_value),
        ],
        0,
    )
    with jax.named_scope("exchange_chips"):
        chips = [send] + [lax.ppermute(send, "wn", [(i, i ^ (2 * k)) for i in range(count)]) for k in (1, 2, 3)]

    part, token = pl.pallas_call(
        sweep_kernel,
        out_shape=(vmem_out(comps, rows, nx, nz), vmem_out(*face_low.shape)),
        in_specs=in_vmem(7),
        out_specs=in_vmem(2),
        scratch_shapes=[VMEM((comps, LANES, LANES), f32)] * 2,
        compiler_params=params,
        cost_estimate=cost(30 * cells, 30 * cells),
        name="sweep",
    )(rhs, edge_low, edge_high, wid, hid, rec, face_low)

    chips = [jnp.where(odd_chip, chips[k ^ 1], chips[k]) for k in range(4)]
    chips = [jnp.where(high_chip, chips[k ^ 2], chips[k]) for k in range(4)]
    low_low = [block[0] for block in chips]
    low_up = [block[1] for block in chips]
    up_up = [block[2] for block in chips]
    resist = [None] + [1.0 / block[3] for block in chips[1:]]
    at_low = [block[4:7] for block in chips]
    at_up = [block[7:10] for block in chips]
    join_01 = 1.0 / (resist[1] + up_up[0] + low_low[1])
    join_23 = 1.0 / (resist[3] + up_up[2] + low_low[3])
    step_01 = at_low[1] - at_up[0]
    step_23 = at_low[3] - at_up[2]
    join_12 = 1.0 / (
        resist[2] + up_up[1] - low_up[1] * low_up[1] * join_01 + low_low[2] - low_up[2] * low_up[2] * join_23
    )
    flow_12 = join_12 * (
        at_low[2] + low_up[2] * join_23 * step_23 - at_up[1] + low_up[1] * join_01 * step_01
    )
    flow_01 = join_01 * (step_01 + low_up[1] * flow_12)
    flow_23 = join_23 * (step_23 + low_up[2] * flow_12)
    flow_up = jnp.where(high_chip, jnp.where(odd_chip, 0.0, flow_23), jnp.where(odd_chip, flow_12, flow_01))
    flow_low = -jnp.where(high_chip, jnp.where(odd_chip, flow_23, flow_12), jnp.where(odd_chip, flow_01, 0.0))
    flow_up = jnp.where(token < 0.0, token, flow_up)
    flow_near = jnp.where(upper_core, flow_up, flow_low)
    flow_far = jnp.where(upper_core, flow_low, flow_up)
    flow_core = join_core * (far_value_in + far_cross * flow_far - near_value_in - cross * flow_near)

    with jax.named_scope("exchange_flux"):
        back = lax.ppermute(
            jnp.concatenate([flow_far, far_push - flow_core], 0), "wn", [(i, i ^ 1) for i in range(count)]
        )
    keep = jnp.concatenate([flow_near, push_in + flow_core], 0)
    whole = jnp.concatenate([jnp.where(upper_core, back, keep), jnp.where(upper_core, keep, back)], 1)
    total_out = whole[:comps] + push_out
    total_in = whole[comps:]
    flux = jnp.concatenate(
        [jnp.where(upper_core, total_in, total_out), jnp.where(upper_core, total_out, total_in)], 0
    )

    chunks = 8
    return pl.pallas_call(
        functools.partial(finish_kernel, chunks),
        out_shape=jax.ShapeDtypeStruct((comps, rows, nx, nz), f32),
        in_specs=in_vmem(4),
        out_specs=hbm,
        scratch_shapes=[VMEM((comps, rows, nx, nz), f32), pltpu.SemaphoreType.DMA((chunks,))],
        compiler_params=params,
        name="finish",
    )(part, left, right, flux)


def solution(mesh):
    placed = (P(None, "wn", None, "xz"), P("wn", None, "xz"))
    return jax.shard_map(
        local, mesh=mesh, in_specs=placed, out_specs=P(None, "wn", None, "xz"), check_vma=False
    )
```
